512 devices in a mesh: row: 32 (over x, y_hi, core), col: 16 (over y_lo, z).
Axes of the slice: x: 4, y: 8 (y_hi: 4, y_lo: 2; y = y_hi * 2 + y_lo), z: 8, core: 2. Of those that a mesh axis runs over, the one named last changes fastest.
Arguments:
- activation: bfloat16 [1024, 12288], P('row', 'col'), may hold values from -6 to 6
- upstream: bfloat16 [1024, 49152], P('col', 'row'), may hold values from -0.75 to 0.75
- up_weight: bfloat16 [12288, 49152], P('col', 'row'), may hold values from -0.0546875 to 0.0546875
Outputs:
- act_gradient: bfloat16 [1024, 12288], P('row', 'col')
- weight_gradient: bfloat16 [12288, 49152], P('col', 'row')
The draws below stay inside these ranges and needn't reach their ends.
All inputs are finite; a program needn't handle non-finite values.
Results may differ from the reference program's by a relative error of at most 0.001.
Values may be sent and summed in bfloat16 or wider, within the bound.
No kernel may reach another device: no remote copies, remote signals or barrier semaphores. Data moves between devices by JAX's collectives and lax.ppermute only.
A program may use at most 64 MiB of HBM per device.

```python
import jax
import jax.numpy as jnp
from jax import lax

D = 12288
FF = 49152
TOKENS = 1024


def strengthened(entries, stream_key, source, target, blocks, factor):
    def block_of(axis_at):
        return (jnp.arange(entries.shape[axis_at]) // (entries.shape[axis_at] // blocks)).reshape((-1,) + (1,) * (entries.ndim - 1 - axis_at))

    one_side = jax.random.permutation(stream_key, blocks)[block_of(target)]
    far = (block_of(target) + blocks // 2) % blocks
    return jnp.where((block_of(source) == one_side) | (block_of(source) == far), factor * entries, entries)


def steps_of(stream_key, dims, shards, low, high):
    level = 1.0
    for position, parts in shards:
        steps = jax.random.uniform(jax.random.fold_in(jax.random.fold_in(stream_key, 6), position), (parts,), jnp.float32, low / len(shards), high / len(shards))
        level = level * jnp.repeat(jnp.exp(steps), dims[position] // parts).reshape((-1,) + (1,) * (len(dims) - 1 - position))
    return level


def bell_draw(key, shape, scale, bound, split=(), held_as=jnp.bfloat16):
    result = scale * jax.random.normal(key, shape, jnp.float32)
    if split:
        result = result * steps_of(key, shape, split, -0.22, 0.18)
    return jnp.clip(result, -bound, bound).astype(held_as)


def bell_draw_with(rng, extent, width, limit, cuts, heavy, dtype=jnp.bfloat16):
    drawn = width * jax.random.normal(rng, extent, jnp.float32)
    if cuts:
        drawn = drawn * steps_of(rng, extent, cuts, -0.22, 0.18)
    return jnp.clip(strengthened(drawn, jax.random.fold_in(rng, 3), *heavy), -limit, limit).astype(dtype)


def setup_inputs(seed: int = 0) -> dict:
    streams_of = jax.random.split(jax.random.key(seed), 4)
    activation = bell_draw(streams_of[0], (TOKENS, D), 1.0, 6.0, ((0, 32), (1, 16)))
    upstream = bell_draw_with(streams_of[1], (TOKENS, FF), 0.125, 0.75, ((0, 16), (1, 32)), (1, 0, 32, 2.75))
    up_weight = bell_draw(streams_of[2], (D, FF), D ** -0.5, 0.0546875, ((0, 16), (1, 32)))
    return {"activation": activation, "upstream": upstream, "up_weight": up_weight}


def reference(activation, upstream, up_weight):
    act_gradient = lax.dot_general(upstream, up_weight, (((1,), (1,)), ((), ())), preferred_element_type=jnp.float32)
    weight_gradient = lax.dot_general(activation, upstream, (((0,), (0,)), ((), ())), preferred_element_type=jnp.float32)
    return act_gradient.astype(jnp.bfloat16), weight_gradient.astype(jnp.bfloat16)
```

```python
import jax
import jax.numpy as jnp
from jax import lax
from jax.experimental import pallas as pl
from jax.experimental.pallas import tpu as pltpu
from jax.sharding import Mesh, PartitionSpec as P

AXES = ("x", "yh", "core", "yl", "z")
ROW = ("x", "yh", "core")
COL = ("yl", "z")


def swap(value, axis):
    return lax.ppermute(value, axis, [(0, 1), (1, 0)])


def partial_kernel(which, grads, weight, out):
    rows = grads[...].reshape(128, 1536)
    out[0] = lax.dot_general(
        rows, weight[...], (((1,), (1,)), ((), ())), preferred_element_type=jnp.float32
    )


def partial_add_kernel(which, grads, weight, other, out):
    rows = grads[...].reshape(128, 1536)
    out[0] = other[0] + lax.dot_general(
        rows, weight[...], (((1,), (1,)), ((), ())), preferred_element_type=jnp.float32
    )


def partial(which, grads, weight, other=None):
    specs = [
        pl.BlockSpec((1, 4, 1, 1, 32, 1536), lambda x, w: (x % 2, 0, x // 2, w[0], 0, 0)),
        pl.BlockSpec((768, 1536), lambda x, w: (0, 0)),
    ]
    block = pl.BlockSpec((1, 128, 768), lambda x, w: (x, 0, 0))
    args = (which, grads, weight)
    if other is not None:
        specs.append(block)
        args += (other,)
    return pl.pallas_call(
        partial_kernel if other is None else partial_add_kernel,
        grid_spec=pltpu.PrefetchScalarGridSpec(
            num_scalar_prefetch=1, grid=(4,), in_specs=specs, out_specs=block
        ),
        out_shape=jax.ShapeDtypeStruct((4, 128, 768), jnp.float32),
        compiler_params=pltpu.CompilerParams(vmem_limit_bytes=32 * 2**20),
        cost_estimate=pl.CostEstimate(
            flops=2 * 512 * 768 * 1536, bytes_accessed=8 * 2**20, transcendentals=0
        ),
    )(*args)


def weight_kernel(act, grads, out, turned):
    @pl.when(pl.program_id(0) == 0)
    def _():
        for core in range(2):
            for yl in range(2):
                turned[core, yl] = act[core, yl].T

    total = jnp.zeros(out.shape, jnp.float32)
    for core in range(2):
        for yl in range(2):
            rows = grads[:, yl, core].reshape(256, out.shape[1])
            total += jnp.dot(turned[core, yl], rows, preferred_element_type=jnp.float32)
    out[...] = total.astype(out.dtype)


def weight_gradient(act, grads):
    wide = 256
    return pl.pallas_call(
        weight_kernel,
        grid=(1536 // wide,),
        in_specs=[
            pl.BlockSpec((2, 2, 256, 768), lambda n: (0, 0, 0, 0)),
            pl.BlockSpec((8, 2, 2, 32, wide), lambda n: (0, 0, 0, 0, n)),
        ],
        out_specs=pl.BlockSpec((768, wide), lambda n: (0, n)),
        out_shape=jax.ShapeDtypeStruct((768, 1536), jnp.bfloat16),
        scratch_shapes=[pltpu.VMEM((2, 2, 768, 256), jnp.bfloat16)],
        compiler_params=pltpu.CompilerParams(vmem_limit_bytes=32 * 2**20),
        cost_estimate=pl.CostEstimate(
            flops=2 * 1024 * 768 * 1536, bytes_accessed=7 * 2**20, transcendentals=0
        ),
    )(act, grads)


def on_device(activation, upstream, up_weight):
    core = lax.axis_index("core").astype(jnp.int32).reshape(1)

    pair = lax.all_gather(upstream, "yl", axis=0, tiled=True)
    grads = lax.all_gather(pair, "z", axis=0, tiled=True)

    act = lax.all_to_all(jnp.tile(activation, (4, 1)), "yh", 0, 0, tiled=True)
    act = lax.all_to_all(jnp.tile(act, (4, 1)), "x", 0, 0, tiled=True)
    sibling = swap(act, "core")
    act = jnp.where(core[0] == 0, jnp.stack([act, sibling]), jnp.stack([sibling, act]))

    blocks = grads.reshape(2, 4, 2, 2, 32, 1536)
    other = swap(partial(1 - core, blocks, up_weight), "core")
    weight_grad = weight_gradient(
        act.reshape(2, 2, 256, 768), grads.reshape(8, 2, 2, 32, 1536)
    )
    total = partial(core, blocks, up_weight, other)
    total = lax.all_to_all(total, "x", 0, 0, tiled=False).sum(0)
    total = lax.all_to_all(total.reshape(4, 32, 768), "yh", 0, 0, tiled=False).sum(0)
    return total.astype(jnp.bfloat16), weight_grad


def solution(mesh):
    fine = Mesh(mesh.devices.reshape(4, 4, 2, 2, 8), AXES)
    return jax.shard_map(
        on_device,
        mesh=fine,
        in_specs=(P(ROW, COL), P(COL, ROW), P(COL, ROW)),
        out_specs=(P(ROW, COL), P(COL, ROW)),
        check_vma=False,
    )
```

```python
import jax
import jax.numpy as jnp
from jax import lax
from jax.experimental import pallas as pl
from jax.experimental.pallas import tpu as pltpu
from jax.sharding import Mesh, PartitionSpec as P

AXES = ("x", "yh", "core", "yl", "z")
ROW = ("x", "yh", "core")
COL = ("yl", "z")
SMEM = pl.BlockSpec(memory_space=pltpu.SMEM)
VMEM = pl.BlockSpec(memory_space=pltpu.VMEM)
MIB = 2**20


def swap(value, axis):
    return lax.ppermute(value, axis, [(0, 1), (1, 0)])


def around(value, axis, sign=1):
    pairs = [
        (2 * i + c, 2 * ((i + sign * (1 - 2 * c)) % 4) + c) for i in range(4) for c in range(2)
    ]
    return lax.ppermute(value, (axis, "core"), pairs)


def sums_kernel(place, weight, grads, *outs):
    rows = []
    for i in range(4):
        x = place[1 + i]
        first = 4 * lax.rem(x, 2)
        rows.append(grads[pl.ds(first, 4), x // 2, place[0]].reshape(128, -1))
    product = jnp.dot(
        jnp.concatenate(rows), weight[...], preferred_element_type=jnp.float32
    ).reshape(4, 4, 32, -1)
    if len(outs) == 1:
        outs[0][...] = product
    else:
        for i, out in enumerate(outs):
            out[...] = product[i]


def sums(place, weight, grads, apart):
    part = jax.ShapeDtypeStruct((4, 32, 768), jnp.float32)
    whole = jax.ShapeDtypeStruct((4, 4, 32, 768), jnp.float32)
    return pl.pallas_call(
        sums_kernel,
        in_specs=[SMEM, VMEM, VMEM],
        out_specs=[VMEM] * 4 if apart else VMEM,
        out_shape=[part] * 4 if apart else whole,
        compiler_params=pltpu.CompilerParams(vmem_limit_bytes=12 * MIB),
        cost_estimate=pl.CostEstimate(
            flops=2 * 512 * 768 * 1536, bytes_accessed=6 * MIB, transcendentals=0
        ),
    )(place, weight, grads)


def turn_kernel(place, act, sibling, out):
    for yl in range(2):
        out[place[0], yl] = act[yl].T
        out[1 - place[0], yl] = sibling[yl].T


def turn(place, act, sibling):
    return pl.pallas_call(
        turn_kernel,
        in_specs=[SMEM, VMEM, VMEM],
        out_specs=VMEM,
        out_shape=jax.ShapeDtypeStruct((2, 2, 768, 256), jnp.bfloat16),
        compiler_params=pltpu.CompilerParams(vmem_limit_bytes=12 * MIB),
    )(place, act, sibling)


def weight_kernel(turned, grads, out):
    total = jnp.zeros(out.shape, jnp.float32)
    for core in range(2):
        for yl in range(2):
            rows = grads[:, yl, core].reshape(256, out.shape[1])
            total += jnp.dot(turned[core, yl], rows, preferred_element_type=jnp.float32)
    out[...] = total.astype(out.dtype)


def weight_gradient(turned, grads):
    wide = 512
    return pl.pallas_call(
        weight_kernel,
        grid=(1536 // wide,),
        in_specs=[
            pl.BlockSpec((2, 2, 768, 256), lambda n: (0, 0, 0, 0)),
            pl.BlockSpec((8, 2, 2, 32, wide), lambda n: (0, 0, 0, 0, n)),
        ],
        out_specs=pl.BlockSpec((768, wide), lambda n: (0, n)),
        out_shape=jax.ShapeDtypeStruct((768, 1536), jnp.bfloat16),
        compiler_params=pltpu.CompilerParams(vmem_limit_bytes=20 * MIB),
        cost_estimate=pl.CostEstimate(
            flops=2 * 1024 * 768 * 1536, bytes_accessed=7 * MIB, transcendentals=0
        ),
    )(turned, grads)


def on_device(activation, upstream, up_weight):
    core, x = lax.axis_index("core"), lax.axis_index("x")
    way = 1 - 2 * core

    pair = lax.all_gather(upstream, "yl", axis=0, tiled=True)
    grads = lax.all_gather(pair, "z", axis=0, tiled=True).reshape(8, 2, 2, 32, 1536)

    weight = up_weight.T
    act = lax.all_to_all(jnp.tile(activation, (4, 1)), "yh", 0, 0, tiled=True)
    act = lax.all_to_all(jnp.tile(act, (4, 1)), "x", 0, 0, tiled=True)
    turned = turn(
        core.astype(jnp.int32).reshape(1),
        act.reshape(2, 256, 768),
        swap(act, "core").reshape(2, 256, 768),
    )
    grads, weight, turned = lax.optimization_barrier((grads, weight, turned))

    def work(half, sign):
        steps = [lax.rem(x + sign * step + 4, 4) for step in range(4)]
        return jnp.stack([half, *steps]).astype(jnp.int32)

    other = swap(sums(work(1 - core, -way), weight, grads, False), "core")
    parts = sums(work(core, way), weight, grads, True)
    own, one, two, three = (part + other[i] for i, part in enumerate(parts))
    passed = around(two, "x")
    direct = around(three, "x", -1)
    total = own + direct + around(one + passed, "x")

    weight_grad = weight_gradient(turned, grads)
    total, weight_grad = lax.optimization_barrier((total, weight_grad))
    total = lax.all_to_all(total, "yh", 0, 0).sum(0)
    return total.astype(jnp.bfloat16), weight_grad


def solution(mesh):
    fine = Mesh(mesh.devices.reshape(4, 4, 2, 2, 8), AXES)
    return jax.shard_map(
        on_device,
        mesh=fine,
        in_specs=(P(ROW, COL), P(COL, ROW), P(COL, ROW)),
        out_specs=(P(ROW, COL), P(COL, ROW)),
        check_vma=False,
    )
```

```python
import functools

import jax
import jax.numpy as jnp
from jax import lax
from jax.experimental import pallas as pl
from jax.experimental.pallas import tpu as pltpu
from jax.sharding import Mesh, PartitionSpec as P

AXES = ("x", "yh", "core", "yl", "z")
ROW = ("x", "yh", "core")
COL = ("yl", "z")
SMEM = pl.BlockSpec(memory_space=pltpu.SMEM)
VMEM = pl.BlockSpec(memory_space=pltpu.VMEM)
MIB = 2**20
HOPS = (0, 1, 2, 3, 4, -1, -2, -3)


def swap(value, axis):
    return lax.ppermute(value, axis, [(0, 1), (1, 0)])


def around(value, axis="z", sign=1):
    n = 8 if axis == "z" else 4
    pairs = []
    for c in range(2):
        for i in range(n):
            j = (i + sign * (1 - 2 * c)) % n
            pairs.append((c * n + i, c * n + j))
    if axis == "z":
        return lax.ppermute(value, ("core", "z"), pairs)
    pairs = [(2 * (i % n) + i // n, 2 * (j % n) + j // n) for i, j in pairs]
    return lax.ppermute(value, (axis, "core"), pairs)


def origin(place, hops):
    return lax.rem(place[1] + (2 * place[0] - 1) * hops + 8, 8)


def sums_kernel(far, place, weight, *refs):
    held, out = refs[:-1], refs[-1]
    half = 1 - place[0] if far else place[0]
    rows = jnp.concatenate([h[:, half].reshape(64, -1) for h in held])
    product = jnp.dot(rows, weight[...], preferred_element_type=jnp.float32)
    for i, hops in enumerate(HOPS):
        z = origin(place, hops)
        for yl in range(2):
            at = 64 * i + 32 * yl
            step = lax.rem((1 - 2 * half) * (2 * yl + z // 4 - place[2]) + 4, 4)
            out[step, lax.rem(z, 4)] = product[at : at + 32]


def sums(far, place, weight, held):
    return pl.pallas_call(
        functools.partial(sums_kernel, far),
        in_specs=[SMEM] + [VMEM] * (1 + len(held)),
        out_specs=VMEM,
        out_shape=jax.ShapeDtypeStruct((4, 4, 32, 768), jnp.float32),
        compiler_params=pltpu.CompilerParams(vmem_limit_bytes=12 * MIB),
        cost_estimate=pl.CostEstimate(
            flops=2 * 512 * 768 * 1536, bytes_accessed=8 * MIB, transcendentals=0
        ),
    )(place, weight, *held)


def flip_kernel(weight, out):
    out[...] = weight[...].T


def flip(weight):
    return pl.pallas_call(
        flip_kernel,
        in_specs=[VMEM],
        out_specs=VMEM,
        out_shape=jax.ShapeDtypeStruct((1536, 768), jnp.bfloat16),
        compiler_params=pltpu.CompilerParams(vmem_limit_bytes=12 * MIB),
        cost_estimate=pl.CostEstimate(flops=0, bytes_accessed=5 * MIB, transcendentals=0),
    )(weight)


def turn_kernel(place, act, sibling, out):
    for yl in range(2):
        out[place[0], yl] = act[yl].T
        out[1 - place[0], yl] = sibling[yl].T


def turn(place, act, sibling):
    return pl.pallas_call(
        turn_kernel,
        in_specs=[SMEM, VMEM, VMEM],
        out_specs=VMEM,
        out_shape=jax.ShapeDtypeStruct((2, 2, 768, 256), jnp.bfloat16),
        compiler_params=pltpu.CompilerParams(vmem_limit_bytes=12 * MIB),
    )(place, act, sibling)


def weight_kernel(place, turned, *refs):
    held, (out, ordered) = refs[: len(HOPS)], refs[len(HOPS) :]
    for block, hops in zip(held, HOPS):
        ordered[origin(place, hops)] = block[...]
    total = jnp.zeros(out.shape, jnp.float32)
    for core in range(2):
        for yl in range(2):
            rows = ordered[:, yl, core].reshape(256, out.shape[1])
            total += jnp.dot(turned[core, yl], rows, preferred_element_type=jnp.float32)
    out[...] = total.astype(out.dtype)


def weight_gradient(place, turned, held):
    wide = 512
    return pl.pallas_call(
        weight_kernel,
        grid=(1536 // wide,),
        in_specs=[SMEM, pl.BlockSpec((2, 2, 768, 256), lambda n: (0, 0, 0, 0))]
        + [pl.BlockSpec((2, 2, 32, wide), lambda n: (0, 0, 0, n))] * len(HOPS),
        out_specs=pl.BlockSpec((768, wide), lambda n: (0, n)),
        out_shape=jax.ShapeDtypeStruct((768, 1536), jnp.bfloat16),
        scratch_shapes=[pltpu.VMEM((8, 2, 2, 32, wide), jnp.bfloat16)],
        compiler_params=pltpu.CompilerParams(vmem_limit_bytes=20 * MIB),
        cost_estimate=pl.CostEstimate(
            flops=2 * 1024 * 768 * 1536, bytes_accessed=7 * MIB, transcendentals=0
        ),
    )(place, turned, *held)


def on_device(activation, upstream, up_weight):
    place = jnp.stack([lax.axis_index(name) for name in ("core", "z", "x")]).astype(jnp.int32)
    upstream, place = lax.optimization_barrier((upstream, place))
    weight = flip(up_weight)

    act = lax.all_to_all(jnp.tile(activation, (16, 1)), ("x", "yh"), 0, 0, tiled=True)
    mine = [lax.all_gather(upstream, "yl", axis=0, tiled=True).reshape(2, 2, 32, 1536)]
    other = [swap(mine[0], "core")]
    for step in range(3):
        mine.append(around(mine[-1]))
        other.append(around(other[-1]))
    mine[2], weight = lax.optimization_barrier((mine[2], weight))
    mine[3] = around(mine[2])
    side = swap(other[1], "core")
    mine[3], side = lax.optimization_barrier((mine[3], side))
    mine.append(around(mine[3]))
    sides = [side, swap(other[2], "core"), swap(other[3], "core")]
    *held, act = lax.optimization_barrier((*mine, *sides, act))

    theirs = swap(sums(True, place, weight, held), "core")
    ours = sums(False, place, weight, held)
    own, one, two, three = (ours[i] + theirs[i] for i in range(4))
    passed = around(two, "x")
    direct = around(three, "x", -1)
    total = own + direct + around(one + passed, "x")

    turned = turn(place, act.reshape(2, 256, 768), swap(act, "core").reshape(2, 256, 768))
    weight_grad = weight_gradient(place, turned, held)
    total, weight_grad = lax.optimization_barrier((total, weight_grad))
    total = lax.all_to_all(total, "yh", 0, 0).sum(0)
    return total.astype(jnp.bfloat16), weight_grad


def solution(mesh):
    fine = Mesh(mesh.devices.reshape(4, 4, 2, 2, 8), AXES)
    return jax.shard_map(
        on_device,
        mesh=fine,
        in_specs=(P(ROW, COL), P(COL, ROW), P(COL, ROW)),
        out_specs=(P(ROW, COL), P(COL, ROW)),
        check_vma=False,
    )
```

```python
import functools

import jax
import jax.numpy as jnp
from jax import lax
from jax.experimental import pallas as pl
from jax.experimental.pallas import tpu as pltpu
from jax.sharding import Mesh, PartitionSpec as P

AXES = ("x", "yh", "core", "yl", "z")
ROW = ("x", "yh", "core")
COL = ("yl", "z")
SMEM = pl.BlockSpec(memory_space=pltpu.SMEM)
VMEM = pl.BlockSpec(memory_space=pltpu.VMEM)
MIB = 2**20
HOPS = (0, 1, 2, 3, 4, -1, -2, -3)


def swap(value, axis):
    return lax.ppermute(value, axis, [(0, 1), (1, 0)])


def around(value, axis="z", sign=1):
    n = 8 if axis == "z" else 4
    pairs = []
    for c in range(2):
        for i in range(n):
            j = (i + sign * (1 - 2 * c)) % n
            pairs.append((c * n + i, c * n + j))
    if axis == "z":
        return lax.ppermute(value, ("core", "z"), pairs)
    pairs = [(2 * (i % n) + i // n, 2 * (j % n) + j // n) for i, j in pairs]
    return lax.ppermute(value, (axis, "core"), pairs)


def origin(place, hops):
    return lax.rem(place[1] + (2 * place[0] - 1) * hops + 8, 8)


def sums_kernel(far, place, weight, *refs):
    held, out = refs[:-1], refs[-1]
    half = 1 - place[0] if far else place[0]
    rows = jnp.concatenate([h[:, half].reshape(64, -1) for h in held])
    product = jnp.dot(rows, weight[...], preferred_element_type=jnp.float32)
    for i, hops in enumerate(HOPS):
        z = origin(place, hops)
        for yl in range(2):
            at = 64 * i + 32 * yl
            step = lax.rem((1 - 2 * half) * (2 * yl + z // 4 - place[2]) + 4, 4)
            out[step, lax.rem(z, 4)] = product[at : at + 32]


def sums(far, place, weight, held):
    return pl.pallas_call(
        functools.partial(sums_kernel, far),
        in_specs=[SMEM] + [VMEM] * (1 + len(held)),
        out_specs=VMEM,
        out_shape=jax.ShapeDtypeStruct((4, 4, 32, 768), jnp.float32),
        compiler_params=pltpu.CompilerParams(vmem_limit_bytes=12 * MIB),
        cost_estimate=pl.CostEstimate(
            flops=2 * 512 * 768 * 1536, bytes_accessed=8 * MIB, transcendentals=0
        ),
    )(place, weight, *held)


def flip_kernel(weight, out):
    out[...] = weight[...].T


def flip(weight):
    return pl.pallas_call(
        flip_kernel,
        in_specs=[VMEM],
        out_specs=VMEM,
        out_shape=jax.ShapeDtypeStruct((1536, 768), jnp.bfloat16),
        compiler_params=pltpu.CompilerParams(vmem_limit_bytes=12 * MIB),
        cost_estimate=pl.CostEstimate(flops=0, bytes_accessed=5 * MIB, transcendentals=0),
    )(weight)


def turn_kernel(place, act, sibling, out):
    for core, rows in ((place[0], act), (1 - place[0], sibling)):
        for yl in range(2):
            blocks = [rows[8 * yl + origin(place, hops)] for hops in HOPS]
            out[core, yl] = jnp.concatenate(blocks).T


def turn(place, act, sibling):
    return pl.pallas_call(
        turn_kernel,
        in_specs=[SMEM, VMEM, VMEM],
        out_specs=VMEM,
        out_shape=jax.ShapeDtypeStruct((2, 2, 768, 256), jnp.bfloat16),
        compiler_params=pltpu.CompilerParams(vmem_limit_bytes=12 * MIB),
        cost_estimate=pl.CostEstimate(flops=0, bytes_accessed=5 * MIB, transcendentals=0),
    )(place, act, sibling)


def weight_kernel(turned, *refs):
    held, out = refs[:-1], refs[-1]
    total = jnp.zeros(out.shape, jnp.float32)
    for core in range(2):
        for yl in range(2):
            rows = jnp.concatenate([block[yl, core] for block in held])
            total += jnp.dot(turned[core, yl], rows, preferred_element_type=jnp.float32)
    out[...] = total.astype(out.dtype)


def weight_gradient(turned, held):
    wide = 512
    return pl.pallas_call(
        weight_kernel,
        grid=(1536 // wide,),
        in_specs=[pl.BlockSpec((2, 2, 768, 256), lambda n: (0, 0, 0, 0))]
        + [pl.BlockSpec((2, 2, 32, wide), lambda n: (0, 0, 0, n))] * len(HOPS),
        out_specs=pl.BlockSpec((768, wide), lambda n: (0, n)),
        out_shape=jax.ShapeDtypeStruct((768, 1536), jnp.bfloat16),
        compiler_params=pltpu.CompilerParams(vmem_limit_bytes=20 * MIB),
        cost_estimate=pl.CostEstimate(
            flops=2 * 1024 * 768 * 1536, bytes_accessed=7 * MIB, transcendentals=0
        ),
    )(turned, *held)


def on_device(activation, upstream, up_weight):
    place = jnp.stack([lax.axis_index(name) for name in ("core", "z", "x")]).astype(jnp.int32)
    upstream, place = lax.optimization_barrier((upstream, place))
    weight = flip(up_weight)

    act = lax.all_to_all(jnp.tile(activation, (16, 1)), ("x", "yh"), 0, 0, tiled=True)
    mine = [lax.all_gather(upstream, "yl", axis=0, tiled=True).reshape(2, 2, 32, 1536)]
    other = [swap(mine[0], "core")]
    for step in range(3):
        mine.append(around(mine[-1]))
        other.append(around(other[-1]))
    mine[2], weight = lax.optimization_barrier((mine[2], weight))
    mine[3] = around(mine[2])
    side = swap(other[1], "core")
    mine[3], side = lax.optimization_barrier((mine[3], side))
    mine.append(around(mine[3]))
    sides = [side, swap(other[2], "core"), swap(other[3], "core")]
    *held, act = lax.optimization_barrier((*mine, *sides, act))
    held = [pltpu.with_memory_space_constraint(block, pltpu.HBM) for block in held]
    act = act.reshape(16, 32, 768)

    theirs = swap(sums(True, place, weight, held), "core")
    ours = sums(False, place, weight, held)
    own, one, two, three = (ours[i] + theirs[i] for i in range(4))
    passed = around(two, "x")
    direct = around(three, "x", -1)
    total = own + direct + around(one + passed, "x")

    weight_grad = weight_gradient(turn(place, act, swap(act, "core")), held)
    total, weight_grad = lax.optimization_barrier((total, weight_grad))
    total = lax.all_to_all(total, "yh", 0, 0).sum(0)
    return total.astype(jnp.bfloat16), weight_grad


def solution(mesh):
    fine = Mesh(mesh.devices.reshape(4, 4, 2, 2, 8), AXES)
    return jax.shard_map(
        on_device,
        mesh=fine,
        in_specs=(P(ROW, COL), P(COL, ROW), P(COL, ROW)),
        out_specs=(P(ROW, COL), P(COL, ROW)),
        check_vma=False,
    )
```

```python
import functools

import jax
import jax.numpy as jnp
from jax import lax
from jax.experimental import pallas as pl
from jax.experimental.pallas import tpu as pltpu
from jax.sharding import Mesh, PartitionSpec as P

AXES = ("x", "yh", "core", "yl", "z")
ROW = ("x", "yh", "core")
COL = ("yl", "z")
SMEM = pl.BlockSpec(memory_space=pltpu.SMEM)
VMEM = pl.BlockSpec(memory_space=pltpu.VMEM)
MIB = 2**20
HOPS = (0, 1, 2, 3, 4, -1, -2, -3)
EARLY, LATE = (0, 1, 2, 3, -1, -2), (4, -3)


def swap(value, axis):
    return lax.ppermute(value, axis, [(0, 1), (1, 0)])


def around(value, axis="z", sign=1):
    n = 8 if axis == "z" else 4
    pairs = []
    for c in range(2):
        for i in range(n):
            j = (i + sign * (1 - 2 * c)) % n
            pairs.append((c * n + i, c * n + j))
    if axis == "z":
        return lax.ppermute(value, ("core", "z"), pairs)
    pairs = [(2 * (i % n) + i // n, 2 * (j % n) + j // n) for i, j in pairs]
    return lax.ppermute(value, (axis, "core"), pairs)


def origin(place, hops):
    return lax.rem(place[1] + (2 * place[0] - 1) * hops + 8, 8)


def sums_kernel(far, arrived, place, weight, *refs):
    held, before, out = refs[: len(arrived)], refs[len(arrived) : -1], refs[-1]
    half = 1 - place[0] if far else place[0]
    rows = jnp.concatenate([h[:, half].reshape(64, -1) for h in held])
    product = jnp.dot(rows, weight[...], preferred_element_type=jnp.float32)
    if before:
        out[...] = before[0][...]
    for i, hops in enumerate(arrived):
        z = origin(place, hops)
        for yl in range(2):
            at = 64 * i + 32 * yl
            step = lax.rem((1 - 2 * half) * (2 * yl + z // 4 - place[2]) + 4, 4)
            out[step, lax.rem(z, 4)] = product[at : at + 32]


def sums(far, arrived, place, weight, held, *before):
    return pl.pallas_call(
        functools.partial(sums_kernel, far, arrived),
        in_specs=[SMEM] + [VMEM] * (1 + len(held) + len(before)),
        out_specs=VMEM,
        out_shape=jax.ShapeDtypeStruct((4, 4, 32, 768), jnp.float32),
        compiler_params=pltpu.CompilerParams(vmem_limit_bytes=12 * MIB),
        cost_estimate=pl.CostEstimate(
            flops=128 * len(held) * 768 * 1536, bytes_accessed=8 * MIB, transcendentals=0
        ),
    )(place, weight, *held, *before)


def flip_kernel(weight, out):
    out[...] = weight[...].T


def flip(weight):
    return pl.pallas_call(
        flip_kernel,
        in_specs=[VMEM],
        out_specs=VMEM,
        out_shape=jax.ShapeDtypeStruct((1536, 768), jnp.bfloat16),
        compiler_params=pltpu.CompilerParams(vmem_limit_bytes=12 * MIB),
        cost_estimate=pl.CostEstimate(flops=0, bytes_accessed=5 * MIB, transcendentals=0),
    )(weight)


def turn_kernel(place, act, sibling, out):
    for core, rows in ((place[0], act), (1 - place[0], sibling)):
        for yl in range(2):
            blocks = [rows[8 * yl + origin(place, hops)] for hops in HOPS]
            out[core, yl] = jnp.concatenate(blocks).T


def turn(place, act, sibling):
    return pl.pallas_call(
        turn_kernel,
        in_specs=[SMEM, VMEM, VMEM],
        out_specs=VMEM,
        out_shape=jax.ShapeDtypeStruct((2, 2, 768, 256), jnp.bfloat16),
        compiler_params=pltpu.CompilerParams(vmem_limit_bytes=12 * MIB),
        cost_estimate=pl.CostEstimate(flops=0, bytes_accessed=5 * MIB, transcendentals=0),
    )(place, act, sibling)


def weight_kernel(turned, *refs):
    held, out = refs[:-1], refs[-1]
    total = jnp.zeros(out.shape, jnp.float32)
    for core in range(2):
        for yl in range(2):
            rows = jnp.concatenate([block[yl, core] for block in held])
            total += jnp.dot(turned[core, yl], rows, preferred_element_type=jnp.float32)
    out[...] = total.astype(out.dtype)


def weight_gradient(turned, held):
    wide = 512
    return pl.pallas_call(
        weight_kernel,
        grid=(1536 // wide,),
        in_specs=[pl.BlockSpec((2, 2, 768, 256), lambda n: (0, 0, 0, 0))]
        + [pl.BlockSpec((2, 2, 32, wide), lambda n: (0, 0, 0, n))] * len(HOPS),
        out_specs=pl.BlockSpec((768, wide), lambda n: (0, n)),
        out_shape=jax.ShapeDtypeStruct((768, 1536), jnp.bfloat16),
        compiler_params=pltpu.CompilerParams(vmem_limit_bytes=20 * MIB),
        cost_estimate=pl.CostEstimate(
            flops=2 * 1024 * 768 * 1536, bytes_accessed=7 * MIB, transcendentals=0
        ),
    )(turned, *held)


def on_device(activation, upstream, up_weight):
    place = jnp.stack([lax.axis_index(name) for name in ("core", "z", "x")]).astype(jnp.int32)
    upstream, place = lax.optimization_barrier((upstream, place))
    weight = flip(up_weight)

    act = lax.all_to_all(jnp.tile(activation, (16, 1)), ("x", "yh"), 0, 0, tiled=True)
    mine = [lax.all_gather(upstream, "yl", axis=0, tiled=True).reshape(2, 2, 32, 1536)]
    other = [swap(mine[0], "core")]
    for step in range(3):
        mine.append(around(mine[-1]))
        other.append(around(other[-1]))
    mine[2], weight = lax.optimization_barrier((mine[2], weight))
    mine[3] = around(mine[2])
    side = swap(other[1], "core")
    mine[3], side = lax.optimization_barrier((mine[3], side))
    mine.append(around(mine[3]))
    sides = [side, swap(other[2], "core"), swap(other[3], "core")]
    fixed = lambda blocks: [pltpu.with_memory_space_constraint(b, pltpu.HBM) for b in blocks]
    sides[1], act = lax.optimization_barrier((sides[1], act))
    start = sums(True, EARLY, place, weight, fixed([*mine[:4], *sides[:2]]))
    *held, start = lax.optimization_barrier((*mine, *sides, start))
    held = fixed(held)
    act = act.reshape(16, 32, 768)

    theirs = swap(sums(True, LATE, place, weight, [held[4], held[7]], start), "core")
    ours = sums(False, HOPS, place, weight, held)
    own, one, two, three = (ours[i] + theirs[i] for i in range(4))
    passed = around(two, "x")
    direct = around(three, "x", -1)
    total = own + direct + around(one + passed, "x")

    weight_grad = weight_gradient(turn(place, act, swap(act, "core")), held)
    total, weight_grad = lax.optimization_barrier((total, weight_grad))
    total = lax.all_to_all(total, "yh", 0, 0).sum(0)
    return total.astype(jnp.bfloat16), weight_grad


def solution(mesh):
    fine = Mesh(mesh.devices.reshape(4, 4, 2, 2, 8), AXES)
    return jax.shard_map(
        on_device,
        mesh=fine,
        in_specs=(P(ROW, COL), P(COL, ROW), P(COL, ROW)),
        out_specs=(P(ROW, COL), P(COL, ROW)),
        check_vma=False,
    )
```

```python
import functools

import jax
import jax.numpy as jnp
from jax import lax
from jax.experimental import pallas as pl
from jax.experimental.pallas import tpu as pltpu
from jax.sharding import Mesh, PartitionSpec as P

AXES = ("x", "yh", "core", "yl", "z")
ROW = ("x", "yh", "core")
COL = ("yl", "z")
SMEM = pl.BlockSpec(memory_space=pltpu.SMEM)
VMEM = pl.BlockSpec(memory_space=pltpu.VMEM)
MIB = 2**20
HOPS = (0, 1, 2, 3, 4, -1, -2, -3)
EARLY, LATE = (0, 1, 2, 3, -1, -2), (4, -3)


def swap(value, axis):
    return lax.ppermute(value, axis, [(0, 1), (1, 0)])


def around(value, axis="z", sign=1):
    n = 8 if axis == "z" else 4
    pairs = []
    for c in range(2):
        for i in range(n):
            j = (i + sign * (1 - 2 * c)) % n
            pairs.append((c * n + i, c * n + j))
    if axis == "z":
        return lax.ppermute(value, ("core", "z"), pairs)
    pairs = [(2 * (i % n) + i // n, 2 * (j % n) + j // n) for i, j in pairs]
    return lax.ppermute(value, (axis, "core"), pairs)


def origin(place, hops):
    return lax.rem(place[1] + (2 * place[0] - 1) * hops + 8, 8)


def sums_kernel(far, arrived, place, weight, *refs):
    held, before, out = refs[: len(arrived)], refs[len(arrived) : -1], refs[-1]
    half = 1 - place[0] if far else place[0]
    rows = jnp.concatenate([h[:, half].reshape(64, -1) for h in held])
    product = jnp.dot(rows, weight[...], preferred_element_type=jnp.float32)
    if before:
        out[...] = before[0][...]
    for i, hops in enumerate(arrived):
        z = origin(place, hops)
        for yl in range(2):
            at = 64 * i + 32 * yl
            step = lax.rem((1 - 2 * half) * (2 * yl + z // 4 - place[2]) + 4, 4)
            out[step, lax.rem(z, 4)] = product[at : at + 32]


def sums(far, arrived, place, weight, held, *before):
    return pl.pallas_call(
        functools.partial(sums_kernel, far, arrived),
        in_specs=[SMEM] + [VMEM] * (1 + len(held) + len(before)),
        out_specs=VMEM,
        out_shape=jax.ShapeDtypeStruct((4, 4, 32, 768), jnp.float32),
        compiler_params=pltpu.CompilerParams(vmem_limit_bytes=12 * MIB),
        cost_estimate=pl.CostEstimate(
            flops=128 * len(held) * 768 * 1536, bytes_accessed=8 * MIB, transcendentals=0
        ),
    )(place, weight, *held, *before)


def flip_kernel(weight, out):
    out[...] = weight[...].T


def flip(weight):
    return pl.pallas_call(
        flip_kernel,
        in_specs=[VMEM],
        out_specs=VMEM,
        out_shape=jax.ShapeDtypeStruct((1536, 768), jnp.bfloat16),
        compiler_params=pltpu.CompilerParams(vmem_limit_bytes=12 * MIB),
        cost_estimate=pl.CostEstimate(flops=0, bytes_accessed=5 * MIB, transcendentals=0),
    )(weight)


def copies_kernel(act, out):
    for i in range(16):
        out[i] = act[...]


def copies(act):
    return pl.pallas_call(
        copies_kernel,
        in_specs=[VMEM],
        out_specs=VMEM,
        out_shape=jax.ShapeDtypeStruct((16, 32, 768), jnp.bfloat16),
        compiler_params=pltpu.CompilerParams(vmem_limit_bytes=8 * MIB),
        cost_estimate=pl.CostEstimate(flops=0, bytes_accessed=MIB, transcendentals=0),
    )(pltpu.with_memory_space_constraint(act, pltpu.HBM))


def turn_kernel(place, act, sibling, out):
    for core, rows in ((place[0], act), (1 - place[0], sibling)):
        for yl in range(2):
            blocks = [rows[8 * yl + origin(place, hops)] for hops in HOPS]
            out[core, yl] = jnp.concatenate(blocks).T


def turn(place, act, sibling):
    return pl.pallas_call(
        turn_kernel,
        in_specs=[SMEM, VMEM, VMEM],
        out_specs=VMEM,
        out_shape=jax.ShapeDtypeStruct((2, 2, 768, 256), jnp.bfloat16),
        compiler_params=pltpu.CompilerParams(vmem_limit_bytes=12 * MIB),
        cost_estimate=pl.CostEstimate(flops=0, bytes_accessed=5 * MIB, transcendentals=0),
    )(place, act, sibling)


def weight_kernel(turned, *refs):
    held, out = refs[:-1], refs[-1]
    total = jnp.zeros(out.shape, jnp.float32)
    for core in range(2):
        for yl in range(2):
            rows = jnp.concatenate([block[yl, core] for block in held])
            total += jnp.dot(turned[core, yl], rows, preferred_element_type=jnp.float32)
    out[...] = total.astype(out.dtype)


def weight_gradient(turned, held):
    wide = 512
    return pl.pallas_call(
        weight_kernel,
        grid=(1536 // wide,),
        in_specs=[pl.BlockSpec((2, 2, 768, 256), lambda n: (0, 0, 0, 0))]
        + [pl.BlockSpec((2, 2, 32, wide), lambda n: (0, 0, 0, n))] * len(HOPS),
        out_specs=pl.BlockSpec((768, wide), lambda n: (0, n)),
        out_shape=jax.ShapeDtypeStruct((768, 1536), jnp.bfloat16),
        compiler_params=pltpu.CompilerParams(vmem_limit_bytes=20 * MIB),
        cost_estimate=pl.CostEstimate(
            flops=2 * 1024 * 768 * 1536, bytes_accessed=7 * MIB, transcendentals=0
        ),
    )(turned, *held)


def on_device(activation, upstream, up_weight):
    place = jnp.stack([lax.axis_index(name) for name in ("core", "z", "x")]).astype(jnp.int32)
    upstream, place = lax.optimization_barrier((upstream, place))
    weight = flip(up_weight)

    act = lax.all_to_all(copies(activation), ("x", "yh"), 0, 0, tiled=True)
    mine = [lax.all_gather(upstream, "yl", axis=0, tiled=True).reshape(2, 2, 32, 1536)]
    other = [swap(mine[0], "core")]
    for step in range(3):
        mine.append(around(mine[-1]))
        other.append(around(other[-1]))
    mine[2], weight = lax.optimization_barrier((mine[2], weight))
    mine[3] = around(mine[2])
    side = swap(other[1], "core")
    mine[3], side = lax.optimization_barrier((mine[3], side))
    mine.append(around(mine[3]))
    sides = [side, swap(other[2], "core"), swap(other[3], "core")]
    fixed = lambda blocks: [pltpu.with_memory_space_constraint(b, pltpu.HBM) for b in blocks]
    sides[1], act = lax.optimization_barrier((sides[1], act))
    start = sums(True, EARLY, place, weight, fixed([*mine[:4], *sides[:2]]))
    *held, start = lax.optimization_barrier((*mine, *sides, start))
    held = fixed(held)

    theirs = swap(sums(True, LATE, place, weight, [held[4], held[7]], start), "core")
    ours = sums(False, HOPS, place, weight, held)
    own, one, two, three = (ours[i] + theirs[i] for i in range(4))
    passed = around(two, "x")
    direct = around(three, "x", -1)
    total = own + direct + around(one + passed, "x")

    weight_grad = weight_gradient(turn(place, act, swap(act, "core")), held)
    total, weight_grad = lax.optimization_barrier((total, weight_grad))
    total = lax.all_to_all(total, "yh", 0, 0).sum(0)
    return total.astype(jnp.bfloat16), weight_grad


def solution(mesh):
    fine = Mesh(mesh.devices.reshape(4, 4, 2, 2, 8), AXES)
    return jax.shard_map(
        on_device,
        mesh=fine,
        in_specs=(P(ROW, COL), P(COL, ROW), P(COL, ROW)),
        out_specs=(P(ROW, COL), P(COL, ROW)),
        check_vma=False,
    )
```

```python
import functools

import jax
import jax.numpy as jnp
from jax import lax
from jax.experimental import pallas as pl
from jax.experimental.pallas import tpu as pltpu
from jax.sharding import Mesh, PartitionSpec as P

AXES = ("x", "yh", "core", "yl", "z")
ROW = ("x", "yh", "core")
COL = ("yl", "z")
SMEM = pl.BlockSpec(memory_space=pltpu.SMEM)
VMEM = pl.BlockSpec(memory_space=pltpu.VMEM)
MIB = 2**20
HOPS = (0, 1, 2, 3, 4, -1, -2, -3)
EARLY, LATE = (0, 1, 2, 3, -1, -2), (4, -3)


def swap(value, axis):
    return lax.ppermute(value, axis, [(0, 1), (1, 0)])


def around(value, axis="z", sign=1):
    n = 8 if axis == "z" else 4
    pairs = []
    for c in range(2):
        for i in range(n):
            j = (i + sign * (1 - 2 * c)) % n
            pairs.append((c * n + i, c * n + j))
    if axis == "z":
        return lax.ppermute(value, ("core", "z"), pairs)
    pairs = [(2 * (i % n) + i // n, 2 * (j % n) + j // n) for i, j in pairs]
    return lax.ppermute(value, (axis, "core"), pairs)


def origin(place, hops):
    return lax.rem(place[1] + (2 * place[0] - 1) * hops + 8, 8)


def sums_kernel(far, arrived, place, weight, *refs):
    held, before, out = refs[: len(arrived)], refs[len(arrived) : -1], refs[-1]
    half = 1 - place[0] if far else place[0]
    rows = jnp.concatenate([h[:, half].reshape(64, -1) for h in held])
    product = jnp.dot(rows, weight[...], preferred_element_type=jnp.float32)
    if before:
        out[...] = before[0][...]
    for i, hops in enumerate(arrived):
        z = origin(place, hops)
        for yl in range(2):
            at = 64 * i + 32 * yl
            step = lax.rem((1 - 2 * half) * (2 * yl + z // 4 - place[2]) + 4, 4)
            out[step, lax.rem(z, 4)] = product[at : at + 32]


def sums(far, arrived, place, weight, held, *before):
    return pl.pallas_call(
        functools.partial(sums_kernel, far, arrived),
        in_specs=[SMEM] + [VMEM] * (1 + len(held) + len(before)),
        out_specs=VMEM,
        out_shape=jax.ShapeDtypeStruct((4, 4, 32, 768), jnp.float32),
        compiler_params=pltpu.CompilerParams(vmem_limit_bytes=12 * MIB),
        cost_estimate=pl.CostEstimate(
            flops=128 * len(held) * 768 * 1536, bytes_accessed=8 * MIB, transcendentals=0
        ),
    )(place, weight, *held, *before)


def flip_kernel(weight, out):
    out[...] = weight[...].T


def flip(weight):
    return pl.pallas_call(
        flip_kernel,
        in_specs=[VMEM],
        out_specs=VMEM,
        out_shape=jax.ShapeDtypeStruct((1536, 768), jnp.bfloat16),
        compiler_params=pltpu.CompilerParams(vmem_limit_bytes=12 * MIB),
        cost_estimate=pl.CostEstimate(flops=0, bytes_accessed=5 * MIB, transcendentals=0),
    )(weight)


def copies_kernel(act, out):
    for i in range(16):
        out[i] = act[...]


def copies(act):
    return pl.pallas_call(
        copies_kernel,
        in_specs=[VMEM],
        out_specs=VMEM,
        out_shape=jax.ShapeDtypeStruct((16, 32, 768), jnp.bfloat16),
        compiler_params=pltpu.CompilerParams(vmem_limit_bytes=8 * MIB),
        cost_estimate=pl.CostEstimate(flops=0, bytes_accessed=MIB, transcendentals=0),
    )(pltpu.with_memory_space_constraint(act, pltpu.HBM))


def turn_kernel(place, act, sibling, out):
    for core, rows in ((place[0], act), (1 - place[0], sibling)):
        for yl in range(2):
            blocks = [rows[8 * yl + origin(place, hops)] for hops in HOPS]
            out[core, yl] = jnp.concatenate(blocks).T


def turn(place, act, sibling):
    return pl.pallas_call(
        turn_kernel,
        in_specs=[SMEM, VMEM, VMEM],
        out_specs=VMEM,
        out_shape=jax.ShapeDtypeStruct((2, 2, 768, 256), jnp.bfloat16),
        compiler_params=pltpu.CompilerParams(vmem_limit_bytes=12 * MIB),
        cost_estimate=pl.CostEstimate(flops=0, bytes_accessed=5 * MIB, transcendentals=0),
    )(place, act, sibling)


def weight_kernel(turned, *refs):
    held, out = refs[:-1], refs[-1]
    total = jnp.zeros(out.shape, jnp.float32)
    for core in range(2):
        for yl in range(2):
            rows = jnp.concatenate([block[yl, core] for block in held])
            total += jnp.dot(turned[core, yl], rows, preferred_element_type=jnp.float32)
    out[...] = total.astype(out.dtype)


def weight_gradient(turned, held):
    wide = 768
    return pl.pallas_call(
        weight_kernel,
        grid=(1536 // wide,),
        in_specs=[pl.BlockSpec((2, 2, 768, 256), lambda n: (0, 0, 0, 0))]
        + [pl.BlockSpec((2, 2, 32, wide), lambda n: (0, 0, 0, n))] * len(HOPS),
        out_specs=pl.BlockSpec((768, wide), lambda n: (0, n)),
        out_shape=jax.ShapeDtypeStruct((768, 1536), jnp.bfloat16),
        compiler_params=pltpu.CompilerParams(vmem_limit_bytes=20 * MIB),
        cost_estimate=pl.CostEstimate(
            flops=2 * 1024 * 768 * 1536, bytes_accessed=7 * MIB, transcendentals=0
        ),
    )(turned, *held)


def on_device(activation, upstream, up_weight):
    place = jnp.stack([lax.axis_index(name) for name in ("core", "z", "x")]).astype(jnp.int32)
    upstream, place = lax.optimization_barrier((upstream, place))
    weight = flip(up_weight)

    act = lax.all_to_all(copies(activation), ("x", "yh"), 0, 0, tiled=True)
    mine = [lax.all_gather(upstream, "yl", axis=0, tiled=True).reshape(2, 2, 32, 1536)]
    other = [swap(mine[0], "core")]
    for step in range(3):
        mine.append(around(mine[-1]))
        other.append(around(other[-1]))
    mine[2], weight = lax.optimization_barrier((mine[2], weight))
    mine[3] = around(mine[2])
    side = swap(other[1], "core")
    mine[3], side = lax.optimization_barrier((mine[3], side))
    mine.append(around(mine[3]))
    sides = [side, swap(other[2], "core"), swap(other[3], "core")]
    fixed = lambda blocks: [pltpu.with_memory_space_constraint(b, pltpu.HBM) for b in blocks]
    sides[1], act = lax.optimization_barrier((sides[1], act))
    start = sums(True, EARLY, place, weight, fixed([*mine[:4], *sides[:2]]))
    *held, start = lax.optimization_barrier((*mine, *sides, start))
    held = fixed(held)

    theirs = swap(sums(True, LATE, place, weight, [held[4], held[7]], start), "core")
    ours = sums(False, HOPS, place, weight, held)
    own, one, two, three = (ours[i] + theirs[i] for i in range(4))
    passed = around(two, "x")
    direct = around(three, "x", -1)
    total = own + direct + around(one + passed, "x")

    weight_grad = weight_gradient(turn(place, act, swap(act, "core")), held)
    total, weight_grad = lax.optimization_barrier((total, weight_grad))
    total = lax.all_to_all(total, "yh", 0, 0).sum(0)
    return total.astype(jnp.bfloat16), weight_grad


def solution(mesh):
    fine = Mesh(mesh.devices.reshape(4, 4, 2, 2, 8), AXES)
    return jax.shard_map(
        on_device,
        mesh=fine,
        in_specs=(P(ROW, COL), P(COL, ROW), P(COL, ROW)),
        out_specs=(P(ROW, COL), P(COL, ROW)),
        check_vma=False,
    )
```
